1024 devices in a mesh: dp: 32 (over x, y), fsdp: 32 (over z, core).
Axes of the slice: x: 4, y: 8, z: 16, core: 2. Of those that a mesh axis runs over, the one named last changes fastest.
Arguments:
- proj_grads: bfloat16 [1024, 4096], P('fsdp'), may hold values from -6 to 6
- inv_factor: bfloat16 [4096, 4096], P('dp'), as said below
- counts: int32 [1024], P('fsdp'), may hold values from 1 to 3
- dests: int32 [1024, 1], P('fsdp'), may hold values from 0 to 31; in each aligned block of 32 rows (0 to 31, 32 to 63, ...) at most 2 rows name the same one
- rows: bfloat16 [1024, 8192], P('fsdp'), may hold values from -6 to 6
- weight: bfloat16 [8192, 16384], P('fsdp', 'dp'), may hold values from -0.0625 to 0.0625
- cotangent: bfloat16 [2048, 16384], P('fsdp', 'dp'), may hold values from -1.1953125 to 1.1953125
Outputs:
- activated: bfloat16 [2048, 16384], P('fsdp', 'dp')
- weight_grad: float32 [8192, 16384], P('fsdp', 'dp')
The draws below stay inside these ranges and needn't reach their ends.
Inputs may be any that keep to these rules, and one draw needn't show every extreme that they name: `dests`: within the 32 examples of one device (aligned blocks), no destination is named more than 2 times, a bound that some block reaches. `inv_factor`: an inverse Cholesky factor: lower triangular with a positive diagonal.
All inputs are finite; a program needn't handle non-finite values.
Results may differ from the reference program's by a relative error of at most 0.0051.
Values may be sent and summed in bfloat16 or wider, within the bound.
No kernel may reach another device: no remote copies, remote signals or barrier semaphores. Data moves between devices by JAX's collectives and lax.ppermute only.
A program may use at most 32 MiB of HBM per device.

```python
import math
import jax
import jax.numpy as jnp
import numpy as np
from jax import lax

D = 8192
FW = 16384
K = 4096
C_DEV = 32
SLOT = 2
R_DEV = 64
ROWS = 2048
CAND = 1024
N_FSDP = 32


def draw_inv_factor(key, part):
    key = jax.random.fold_in(key, 7)
    key_body, key_diag, key_scale = jax.random.split(key, 3)
    index = jnp.arange(K)
    lower = (index[:, None] > index[None, :]).astype(jnp.float32)
    entries = jax.random.normal(key_body, (K, K), jnp.float32)
    spread_rows = 0.5 / jnp.sqrt(jnp.maximum(index, 1).astype(jnp.float32))
    below = entries * lower * spread_rows[:, None]
    diag_values = jax.random.uniform(key_diag, (K,), jnp.float32, 1.0, 2.0)
    level = jax.random.uniform(key_scale, (K,), jnp.float32, 0.0, 1.0)
    row_scale = jnp.exp(2.302585 * level) * jnp.exp(1.0986123 * index.astype(jnp.float32) / K)
    factor = (below + jnp.diag(diag_values)) * row_scale[:, None]
    return factor.astype(jnp.bfloat16)


def touch_ends(drawn, own_key, smallest, top_value):
    longest = drawn.shape.index(max(drawn.shape))
    spots = []
    for shift in (0, 1):
        where = [jax.random.randint(jax.random.fold_in(own_key, axis), (), 0, length) for axis, length in enumerate(drawn.shape)]
        where[longest] = (where[longest] + shift) % drawn.shape[longest]
        spots.append(tuple(where))
    return drawn.at[spots[0]].set(smallest).at[spots[1]].set(top_value)


def steps_of(rng, shape, cuts, low, high):
    def one(dim, blocks):
        heights = jax.random.uniform(jax.random.fold_in(jax.random.fold_in(rng, 6), dim), (blocks,), jnp.float32, low / len(cuts), high / len(cuts))
        return jnp.repeat(jnp.exp(heights), shape[dim] // blocks).reshape((-1,) + (1,) * (len(shape) - dim - 1))

    level = one(*cuts[0])
    for cut in cuts[1:]:
        level = level * one(*cut)
    return level


def deal_out(stream_key, own, number, rows, count, top, most, skew):
    sequence = jax.random.permutation(stream_key, count)
    packed, ordinary = shares(count, rows * top, most, skew, True), shares(count, rows * top, most, skew, False)
    places = jnp.arange(count)

    def named(sizes, offset_by):
        used = int((sizes > 0).sum())
        fixed = max(1, used // 4)
        moved = fixed + (places - fixed + offset_by * (used - fixed)) % max(1, count - fixed)
        return jnp.zeros((count,), jnp.int32).at[sequence[jnp.where(places < fixed, places, moved)]].set(jnp.asarray(sizes, jnp.int32))

    sizes = jnp.where(number % 4 == 0, named(packed, number // 4), named(ordinary, number - number // 4 - 1))
    mixed = jax.random.permutation(jax.random.fold_in(own, 3), count)
    giver, sink = mixed[0:count // 2 * 2:2], mixed[1:count // 2 * 2:2]
    slack = jnp.minimum(sizes[giver] - 1, most - sizes[sink]) // 2
    slack = jnp.where((giver == sequence[0]) | (sink == sequence[0]) | (sizes[sink] == 0), 0, jnp.maximum(slack, 0))
    moved = jax.random.randint(jax.random.fold_in(own, 4), (count // 2,), 0, 1 << 20) % (slack + 1)
    sizes = sizes.at[giver].add(-moved).at[sink].add(moved)
    items = jnp.searchsorted(jnp.cumsum(sizes), jnp.arange(rows * top), side="right").astype(jnp.int32)
    table = items.reshape(top, rows).T
    table = table[jax.random.permutation(jax.random.fold_in(own, 1), rows)]
    offset_by = jax.random.randint(jax.random.fold_in(own, 2), (rows, 1), 0, top)
    return jnp.take_along_axis(table, (jnp.arange(top)[None, :] + offset_by) % top, axis=1)


def shares(count, total, most, lean, full):
    loads = [(1 << 20) // math.isqrt(standing ** lean) + 1 for standing in range(1, count + 1)]
    largest = most if full else min(most, max(-(-total // count), total * loads[0] // sum(loads)))
    least = 1 if total - largest >= count - 1 else 0
    given, spare = [largest] + [least] * (count - 1), total - largest - least * (count - 1)
    while spare > 0:
        free = [i for i in range(1, count) if given[i] < largest] or [i for i in range(1, count) if given[i] < most]
        pool, left = sum([loads[i] for i in free]), spare
        for i in free:
            more = min(most - given[i], max(1, left * loads[i] // pool), spare)
            given[i] = given[i] + more
            spare = spare - more
    return np.array(given)


def bell_draw(stream_key, extent, spread, most, cuts=(), held_as=jnp.bfloat16):
    result = spread * jax.random.normal(stream_key, extent, jnp.float32)
    if cuts:
        result = result * steps_of(stream_key, extent, cuts, -0.22, 0.18)
    return jnp.clip(result, -most, most).astype(held_as)


def setup_inputs(seed: int = 0) -> dict:
    arg_keys = jax.random.split(jax.random.key(seed), 8)
    proj_grads = bell_draw(arg_keys[0], (CAND, K), 1.0, 6.0, ((0, 32),))
    inv_factor = draw_inv_factor(jax.random.fold_in(arg_keys[7], 71), 0)
    counts = touch_ends(jax.random.randint(arg_keys[2], (CAND,), 1, 4), jax.random.fold_in(arg_keys[2], 1), 1, 3).astype(jnp.int32)
    dests_keys = jax.random.split(jax.random.fold_in(arg_keys[3], 1), CAND // C_DEV)
    dests_turns = jax.random.permutation(jax.random.fold_in(arg_keys[3], 3), CAND // C_DEV)
    dests = jax.vmap(lambda own, number: deal_out(jax.random.fold_in(arg_keys[3], 2), own, number, C_DEV, N_FSDP, 1, 2 * C_DEV // N_FSDP, 1))(dests_keys, dests_turns).reshape((CAND, 1))
    rows = bell_draw(arg_keys[4], (CAND, D), 1.0, 6.0, ((0, 32),))
    weight = bell_draw(arg_keys[5], (D, FW), D ** -0.5, 0.0625, ((0, 32), (1, 32)))
    cotangent = bell_draw(arg_keys[6], (ROWS, FW), 0.2, 1.1953125, ((0, 32), (1, 32)))
    return {"proj_grads": proj_grads, "inv_factor": inv_factor, "counts": counts, "dests": dests, "rows": rows, "weight": weight, "cotangent": cotangent}


def reference(proj_grads, inv_factor, counts, dests, rows, weight, cotangent):
    projected = jnp.dot(proj_grads, inv_factor.T, preferred_element_type=jnp.float32)
    scores = jnp.sum(projected * projected, axis=1)
    importance = (counts.astype(jnp.float32) * K / scores).astype(jnp.bfloat16)
    target = dests[:, 0].astype(jnp.int32)
    dest_hot = (target[:, None] == jnp.arange(N_FSDP, dtype=jnp.int32)[None, :]).astype(jnp.int32)
    blocked = dest_hot.reshape(N_FSDP, C_DEV, N_FSDP)
    earlier = jnp.cumsum(blocked, axis=1) - blocked
    slot_rank = jnp.sum(earlier * blocked, axis=2).reshape(CAND)
    source = (jnp.arange(CAND, dtype=jnp.int32) // C_DEV).astype(jnp.int32)
    position = (target * R_DEV + source * SLOT + slot_rank).astype(jnp.int32)
    placer = (position[None, :] == jnp.arange(ROWS, dtype=jnp.int32)[:, None])
    placed = jnp.dot(placer.astype(jnp.bfloat16), rows, preferred_element_type=jnp.float32).astype(jnp.bfloat16)
    slot_weight = jnp.dot(placer.astype(jnp.float32), importance.astype(jnp.float32), precision=lax.Precision.HIGHEST)
    hidden = jnp.dot(placed, weight, preferred_element_type=jnp.float32)
    squash = jax.nn.sigmoid(hidden)
    activated = (hidden * squash).astype(jnp.bfloat16)
    grad_hidden = (slot_weight[:, None] * cotangent.astype(jnp.float32) * squash * (1.0 + hidden * (1.0 - squash))).astype(jnp.bfloat16)
    weight_grad = lax.dot_general(placed, grad_hidden, (((0,), (0,)), ((), ())), preferred_element_type=jnp.float32)
    return activated, weight_grad
```

```python
import jax
import jax.numpy as jnp
from jax import lax
from jax.sharding import Mesh, PartitionSpec as P

BF = jnp.bfloat16
F32 = jnp.float32
SWAP = [(0, 1), (1, 0)]


def both(flag, own, other, axis):
    return jnp.where(flag == 0, jnp.stack([own, other], axis), jnp.stack([other, own], axis))


def at(array, index, axis):
    return lax.dynamic_index_in_dim(array, index, axis, keepdims=False)


def butterfly(value, axis):
    size, step = lax.axis_size(axis), 1
    while step < size:
        value = value + lax.ppermute(value, axis, [(i, i ^ step) for i in range(size)])
        step *= 2
    return value


def shards(proj_grads, inv_factor, counts, dests, rows, weight, cotangent):
    nx, nj = lax.axis_size("x"), lax.axis_size("j")
    nz = 2 * nj
    groups = 2 * nz
    x, j, b, c = (lax.axis_index(a) for a in "xjbc")
    z = 2 * j + b
    local, width = rows.shape
    piece, cols = weight.shape
    quad = 4 * piece

    by_source = cotangent.reshape(nz, 2, 2, cols)
    cot_other = lax.ppermute(at(by_source, 1 - c, 1), "c", SWAP)
    cot_chip = both(c, at(by_source, c, 1), cot_other, 0).reshape(2 * groups, cols)
    target = dests[:, 0]
    dest_hot = (target[:, None] == jnp.arange(groups, dtype=jnp.int32)[None, :]).astype(jnp.int32)
    order = jnp.arange(local, dtype=jnp.int32)
    earlier = (order[:, None] > order[None, :]).astype(jnp.int32)
    rank = jnp.sum(jnp.dot(earlier, dest_hot) * dest_hot, axis=1)
    code = (2 * target + rank).astype(BF)
    code_rows = jnp.zeros((8, cols), BF).at[0, :local].set(code)
    gathered = lax.all_gather(
        jnp.concatenate([cot_chip, code_rows], 0), ("j", "b"), axis=0, tiled=False
    )

    share = local // nx
    mine = lax.dynamic_slice_in_dim(rows, x * share, share, 0)
    mine = mine.reshape(share, nj, quad).transpose(1, 0, 2)
    came = lax.all_to_all(mine, "j", 0, 0, tiled=True)
    x_class = lax.all_gather(came, "x", axis=1, tiled=True).reshape(nj * local, quad)

    w_pair = both(b, weight, lax.ppermute(weight, "b", SWAP), 0)
    w_quad = both(c, w_pair, lax.ppermute(w_pair, "c", SWAP), 1).reshape(quad, cols)

    partial = jnp.dot(x_class, w_quad, preferred_element_type=F32).astype(BF)
    partial = lax.all_to_all(partial.reshape(nj, local, cols), "j", 0, 0, tiled=True)
    hidden = jnp.sum(partial.astype(F32), axis=0)

    projected = lax.dot_general(
        proj_grads, inv_factor, (((1,), (1,)), ((), ())), preferred_element_type=F32
    )
    scores = butterfly(butterfly(jnp.sum(projected * projected, axis=1), "x"), "y")
    importance = (counts.astype(F32) * proj_grads.shape[1] / scores).astype(BF)

    payload = jnp.concatenate(
        [hidden.astype(BF), jnp.broadcast_to(importance[:, None], (local, 128))], 1
    )
    payload = lax.all_gather(payload, ("j", "b"), axis=0, tiled=True)
    hid = payload[:, :cols]
    imp = payload[:, cols : cols + 1].astype(F32)

    codes = gathered[:, 2 * groups, :local].astype(jnp.int32)
    from_z = jnp.arange(nz, dtype=jnp.int32)[:, None]
    place = ((codes // 2) * groups + 2 * from_z + codes % 2).reshape(nz * local)
    slots = jnp.arange(nz * 2 * groups, dtype=jnp.int32)
    hot = (slots[:, None] == place[None, :]).astype(BF)
    cot_slots = gathered[:, : 2 * groups].reshape(nz * 2 * groups, cols)
    cot = lax.dot_general(hot, cot_slots, (((0,), (0,)), ((), ())), preferred_element_type=F32)

    hf = hid.astype(F32)
    squash = jax.nn.sigmoid(hf)
    grad_own = (imp * cot * squash * (1.0 + hf * (1.0 - squash))).astype(BF)
    grad_other = lax.ppermute(grad_own, "c", SWAP)

    x_blocks = x_class.reshape(nj, local, 2, 2 * piece)
    x_pair = lax.ppermute(at(x_blocks, 1 - b, 2), "b", SWAP)
    x_chip = both(b, at(x_blocks, b, 2), x_pair, 1).reshape(nz * local, 2, piece)
    x_own = at(x_chip, c, 1)
    x_other = lax.ppermute(at(x_chip, 1 - c, 1), "c", SWAP)
    over_rows = (((0,), (0,)), ((), ()))
    weight_grad = lax.dot_general(x_own, grad_own, over_rows, preferred_element_type=F32)
    weight_grad = weight_grad + lax.dot_general(
        x_other, grad_other, over_rows, preferred_element_type=F32
    )

    chip_slots = jnp.arange(2 * groups, dtype=jnp.int32) + z * 2 * groups
    pick = (chip_slots[:, None] == place[None, :]).astype(BF)
    at_slots = jnp.dot(pick, hid, preferred_element_type=F32)
    act = (at_slots * jax.nn.sigmoid(at_slots)).astype(BF).reshape(2, nz, 2, cols)
    act_other = lax.ppermute(at(act, 1 - c, 0), "c", SWAP)
    activated = both(c, at(act, c, 0), act_other, 1).reshape(2 * groups, cols)
    return activated, weight_grad


def solution(mesh, nx=4):
    dp, fsdp = mesh.devices.shape
    fine = Mesh(mesh.devices.reshape(nx, dp // nx, fsdp // 4, 2, 2), ("x", "y", "j", "b", "c"))
    dp, fsdp = ("x", "y"), ("j", "b", "c")
    in_specs = (
        P(fsdp, None),
        P(dp, None),
        P(fsdp),
        P(fsdp, None),
        P(fsdp, None),
        P(fsdp, dp),
        P(fsdp, dp),
    )
    out_specs = (P(fsdp, dp), P(fsdp, dp))
    return jax.shard_map(shards, mesh=fine, in_specs=in_specs, out_specs=out_specs, check_vma=False)
```

```python
import jax
import jax.numpy as jnp
from jax import lax
from jax.sharding import Mesh, PartitionSpec as P

BF = jnp.bfloat16
F32 = jnp.float32
SWAP = [(0, 1), (1, 0)]


def both(flag, own, other, axis):
    return jnp.where(flag == 0, jnp.stack([own, other], axis), jnp.stack([other, own], axis))


def shards(proj_grads, inv_factor, counts, dests, rows, weight, cotangent):
    nz = lax.axis_size("z")
    nj, groups = nz // 2, 2 * nz
    z, c = lax.axis_index("z"), lax.axis_index("c")
    b = z % 2
    fsdp = ("z", "c")
    local, width = rows.shape
    piece, cols = weight.shape
    quad = 4 * piece
    stride2 = [[2 * i + k for i in range(nj)] for k in range(2)]
    flip = [(i, i ^ 1) for i in range(nz)]

    cot_slots = lax.all_gather(cotangent, fsdp, axis=0, tiled=True)

    sent = rows.reshape(local, nj, quad).transpose(1, 0, 2)
    came = lax.all_to_all(sent, "z", 0, 0, tiled=True, axis_index_groups=stride2)

    projected = lax.dot_general(
        proj_grads, inv_factor, (((1,), (1,)), ((), ())), preferred_element_type=F32
    )
    scores = lax.psum(lax.psum(jnp.sum(projected * projected, axis=1), "x"), "y")
    came, scores = lax.optimization_barrier((came, scores))
    x_class = came.reshape(nj * local, quad)

    w_pair = both(b, weight, lax.ppermute(weight, "z", flip), 0)
    w_quad = both(c, w_pair, lax.ppermute(w_pair, "c", SWAP), 1).reshape(quad, cols)

    partial = jnp.dot(x_class, w_quad, preferred_element_type=F32).astype(BF)

    blocks = [
        lax.dynamic_slice_in_dim(x_class, (2 * bb + cc) * piece, piece, 1)
        for bb, cc in ((b, c), (1 - b, c), (b, 1 - c), (1 - b, 1 - c))
    ]
    _, *blocks = lax.optimization_barrier((partial[:8, :128], *blocks))
    x_own = blocks[0]
    x_b = lax.ppermute(blocks[1], "z", flip)
    x_c = lax.ppermute(blocks[2], "c", SWAP)
    x_bc = lax.ppermute(blocks[3], fsdp, [(i, i ^ 3) for i in range(groups)])

    partial = lax.all_to_all(
        partial.reshape(nj, local, cols), "z", 0, 0, tiled=True, axis_index_groups=stride2
    )
    hidden = jnp.sum(partial.astype(F32), axis=0)

    importance = (counts.astype(F32) * proj_grads.shape[1] / scores).astype(BF)

    target = dests[:, 0]
    dest_hot = (target[:, None] == jnp.arange(groups, dtype=jnp.int32)[None, :]).astype(jnp.int32)
    order = jnp.arange(local, dtype=jnp.int32)
    earlier = (order[:, None] > order[None, :]).astype(jnp.int32)
    rank = jnp.sum(jnp.dot(earlier, dest_hot) * dest_hot, axis=1)
    code = (2 * target + rank).astype(BF)

    lane = jnp.arange(128)[None, :]
    extra = jnp.where(lane == 0, importance[:, None], code[:, None])
    payload = jnp.concatenate([hidden.astype(BF), extra], 1)
    own = lax.all_gather(payload, "z", axis=0, tiled=True)
    other = lax.ppermute(own, "c", SWAP)

    def place_of(part, parity):
        codes = part[:, cols + 1].astype(jnp.int32)
        from_z = jnp.arange(nz * local, dtype=jnp.int32) // local
        return (codes // 2) * (2 * groups) + (2 * from_z + parity) * 2 + codes % 2

    def grad_of(part, place):
        hf = part[:, :cols].astype(F32)
        imp = part[:, cols : cols + 1].astype(F32)
        slots = jnp.arange(2 * groups * groups, dtype=jnp.int32)
        hot = (slots[:, None] == place[None, :]).astype(BF)
        cot = lax.dot_general(hot, cot_slots, (((0,), (0,)), ((), ())), preferred_element_type=F32)
        squash = jax.nn.sigmoid(hf)
        grad = (imp * cot * squash * (1.0 + hf * (1.0 - squash))).astype(BF)
        return grad.reshape(nj, 2, local, cols)

    def product(x_same, x_flip, grad):
        out = 0.0
        for x_part, bb in ((x_same, b), (x_flip, 1 - b)):
            grad_part = lax.dynamic_index_in_dim(grad, bb, 1, keepdims=False)
            out = out + lax.dot_general(
                x_part,
                grad_part.reshape(nj * local, cols),
                (((0,), (0,)), ((), ())),
                preferred_element_type=F32,
            )
        return out

    def picked(part, place):
        mine = jnp.arange(2 * groups, dtype=jnp.int32) + (2 * z + c) * 2 * groups
        pick = (mine[:, None] == place[None, :]).astype(BF)
        return jnp.dot(pick, part[:, :cols], preferred_element_type=F32)

    place_own, place_other = place_of(own, c), place_of(other, 1 - c)
    weight_grad = product(x_own, x_b, grad_of(own, place_own))
    weight_grad = weight_grad + product(x_c, x_bc, grad_of(other, place_other))
    at_slots = picked(own, place_own) + picked(other, place_other)
    activated = (at_slots * jax.nn.sigmoid(at_slots)).astype(BF)
    return activated, weight_grad


def solution(mesh, nx=4):
    dp, fsdp = mesh.devices.shape
    fine = Mesh(mesh.devices.reshape(nx, dp // nx, fsdp // 2, 2), ("x", "y", "z", "c"))
    dp, fsdp = ("x", "y"), ("z", "c")
    in_specs = (
        P(fsdp, None),
        P(dp, None),
        P(fsdp),
        P(fsdp, None),
        P(fsdp, None),
        P(fsdp, dp),
        P(fsdp, dp),
    )
    out_specs = (P(fsdp, dp), P(fsdp, dp))
    return jax.shard_map(shards, mesh=fine, in_specs=in_specs, out_specs=out_specs, check_vma=False)
```

```python
import jax
import jax.numpy as jnp
from jax import lax
from jax.sharding import Mesh, PartitionSpec as P

BF = jnp.bfloat16
F32 = jnp.float32
SWAP = [(0, 1), (1, 0)]


def both(flag, own, other, axis):
    return jnp.where(flag == 0, jnp.stack([own, other], axis), jnp.stack([other, own], axis))


def at(array, index):
    return lax.dynamic_index_in_dim(array, index, 0, keepdims=False)


def shards(proj_grads, inv_factor, counts, dests, rows, weight, cotangent):
    nx, nz = lax.axis_size("x"), lax.axis_size("z")
    nj, groups = nz // 2, 2 * nz
    z, c = lax.axis_index("z"), lax.axis_index("c")
    b = z % 2
    fsdp = ("z", "c")
    local, width = rows.shape
    piece, cols = weight.shape
    quad = 4 * piece
    stride2 = [[2 * i + k for i in range(nj)] for k in range(2)]
    flip = [(i, i ^ 1) for i in range(nz)]

    cot_slots = lax.all_gather(cotangent, fsdp, axis=0, tiled=True)

    w_chip = both(c, weight, lax.ppermute(weight, "c", SWAP), 0)
    w_quad = both(b, w_chip, lax.ppermute(w_chip, "z", flip), 0).reshape(quad, cols)

    share = local // nx
    sent = lax.dynamic_slice_in_dim(rows, lax.axis_index("x") * share, share, 0)
    sent = sent.reshape(share, nj, quad).transpose(1, 0, 2)
    came = lax.all_to_all(sent, "z", 0, 0, tiled=True, axis_index_groups=stride2)

    projected = lax.dot_general(
        proj_grads, inv_factor, (((1,), (1,)), ((), ())), preferred_element_type=F32
    )
    score = jnp.sum(projected * projected, axis=1)
    high = lax.reduce_precision(score, 8, 7)
    middle = lax.reduce_precision(score - high, 8, 7)
    low = score - high - middle
    thirds = jnp.concatenate([high, middle, low, jnp.zeros(quad - 3 * local, F32)]).astype(BF)
    thirds = jnp.broadcast_to(thirds[None, None, :], (1, share, quad))

    came = lax.all_gather(jnp.concatenate([came, thirds], 0), "x", axis=1, tiled=True)
    x_class = came[:nj].reshape(nj * local, quad)
    thirds = came[nj].reshape(nx, share, quad)[:, 0, : 3 * local].astype(F32)
    score = jnp.sum(thirds.reshape(nx * 3, local), axis=0)

    partial = jnp.dot(x_class, w_quad, preferred_element_type=F32).astype(BF)

    blocks = [
        lax.dynamic_slice_in_dim(x_class, 2 * bb * piece, 2 * piece, 1) for bb in (b, 1 - b)
    ]
    _, score, *blocks = lax.optimization_barrier((partial[:8, :128], score, *blocks))
    x_same, x_flip = blocks[0], lax.ppermute(blocks[1], "z", flip)
    scores = lax.psum(score, "y")

    partial = lax.all_to_all(
        partial.reshape(nj, local, cols), "z", 0, 0, tiled=True, axis_index_groups=stride2
    )
    hidden = jnp.sum(partial.astype(F32), axis=0)

    importance = (counts.astype(F32) * proj_grads.shape[1] / scores).astype(BF)

    target = dests[:, 0]
    dest_hot = (target[:, None] == jnp.arange(groups, dtype=jnp.int32)[None, :]).astype(jnp.int32)
    order = jnp.arange(local, dtype=jnp.int32)
    earlier = (order[:, None] > order[None, :]).astype(jnp.int32)
    rank = jnp.sum(jnp.dot(earlier, dest_hot) * dest_hot, axis=1)
    code = (2 * target + rank).astype(BF)

    lane = jnp.arange(128)[None, :]
    extra = jnp.where(lane == 0, importance[:, None], code[:, None])
    payload = jnp.concatenate([hidden.astype(BF), extra], 1)
    part = lax.all_gather(payload, "z", axis=0, tiled=True)

    codes = part[:, cols + 1].astype(jnp.int32)
    from_z = jnp.arange(nz * local, dtype=jnp.int32) // local
    place = (codes // 2) * (2 * groups) + (2 * from_z + c) * 2 + codes % 2

    slots = jnp.arange(4 * groups, dtype=jnp.int32) + 4 * z * groups
    pick = (slots[:, None] == place[None, :]).astype(BF)
    at_slots = jnp.dot(pick, part[:, :cols], preferred_element_type=F32)
    act = (at_slots * jax.nn.sigmoid(at_slots)).astype(BF).reshape(2, 2 * groups, cols)
    act_other = lax.ppermute(at(act, 1 - c), "c", SWAP)
    activated = at(act, c) + act_other

    hf = part[:, :cols].astype(F32)
    imp = part[:, cols : cols + 1].astype(F32)
    slots = jnp.arange(2 * groups * groups, dtype=jnp.int32)
    hot = (slots[:, None] == place[None, :]).astype(BF)
    cot = lax.dot_general(hot, cot_slots, (((0,), (0,)), ((), ())), preferred_element_type=F32)
    squash = jax.nn.sigmoid(hf)
    grad = (imp * cot * squash * (1.0 + hf * (1.0 - squash))).astype(BF)
    grad = grad.reshape(nj, 2, local, cols)

    def product(core):
        out = 0.0
        for x_part, bb in ((x_same, b), (x_flip, 1 - b)):
            x_block = lax.dynamic_slice_in_dim(x_part, core * piece, piece, 1)
            grad_part = lax.dynamic_index_in_dim(grad, bb, 1, keepdims=False)
            out = out + lax.dot_general(
                x_block,
                grad_part.reshape(nj * local, cols),
                (((0,), (0,)), ((), ())),
                preferred_element_type=F32,
            )
        return out

    other = lax.ppermute(product(1 - c).astype(BF), "c", SWAP)
    weight_grad = product(c) + other.astype(F32)
    return activated, weight_grad


def solution(mesh, nx=4):
    dp, fsdp = mesh.devices.shape
    fine = Mesh(mesh.devices.reshape(nx, dp // nx, fsdp // 2, 2), ("x", "y", "z", "c"))
    dp, fsdp = ("x", "y"), ("z", "c")
    in_specs = (
        P(fsdp, None),
        P(dp, None),
        P(fsdp),
        P(fsdp, None),
        P(fsdp, None),
        P(fsdp, dp),
        P(fsdp, dp),
    )
    out_specs = (P(fsdp, dp), P(fsdp, dp))
    return jax.shard_map(shards, mesh=fine, in_specs=in_specs, out_specs=out_specs, check_vma=False)
```

```python
import jax
import jax.numpy as jnp
from jax import lax
from jax.sharding import Mesh, PartitionSpec as P

BF = jnp.bfloat16
F32 = jnp.float32
SWAP = [(0, 1), (1, 0)]


def both(flag, own, other, axis):
    return jnp.where(flag == 0, jnp.stack([own, other], axis), jnp.stack([other, own], axis))


def at(array, index):
    return lax.dynamic_index_in_dim(array, index, 0, keepdims=False)


def shards(proj_grads, inv_factor, counts, dests, rows, weight, cotangent):
    nx, nz = lax.axis_size("x"), lax.axis_size("z")
    nj, groups = nz // 2, 2 * nz
    z, c = lax.axis_index("z"), lax.axis_index("c")
    b = z % 2
    fsdp = ("z", "c")
    local, width = rows.shape
    piece, cols = weight.shape
    quad = 4 * piece
    stride2 = [[2 * i + k for i in range(nj)] for k in range(2)]
    flip = [(i, i ^ 1) for i in range(nz)]

    cot_slots = lax.all_gather(cotangent, fsdp, axis=0, tiled=True)

    w_pair = both(b, weight, lax.ppermute(weight, "z", flip), 0)
    w_quad = both(c, w_pair, lax.ppermute(w_pair, "c", SWAP), 1).reshape(quad, cols)

    share = local // nx
    sent = lax.dynamic_slice_in_dim(rows, lax.axis_index("x") * share, share, 0)
    sent = sent.reshape(share, nj, quad).transpose(1, 0, 2)
    came = lax.all_to_all(sent, "z", 0, 0, tiled=True, axis_index_groups=stride2)

    projected = lax.dot_general(
        proj_grads, inv_factor, (((1,), (1,)), ((), ())), preferred_element_type=F32
    )
    score = jnp.sum(projected * projected, axis=1)
    high = lax.reduce_precision(score, 8, 7)
    middle = lax.reduce_precision(score - high, 8, 7)
    low = score - high - middle
    thirds = jnp.concatenate([high, middle, low, jnp.zeros(quad - 3 * local, F32)]).astype(BF)
    thirds = jnp.broadcast_to(thirds[None, None, :], (1, share, quad))

    came = lax.all_gather(jnp.concatenate([came, thirds], 0), "x", axis=1, tiled=True)
    x_class = came[:nj].reshape(nj * local, quad)
    thirds = came[nj].reshape(nx, share, quad)[:, 0, : 3 * local].astype(F32)
    score = jnp.sum(thirds.reshape(nx * 3, local), axis=0)

    partial = jnp.dot(x_class, w_quad, preferred_element_type=F32).astype(BF)

    blocks = [
        lax.dynamic_slice_in_dim(x_class, 2 * bb * piece, 2 * piece, 1) for bb in (b, 1 - b)
    ]
    _, score, *blocks = lax.optimization_barrier((partial[:8, :128], score, *blocks))
    x_same, x_flip = blocks[0], lax.ppermute(blocks[1], "z", flip)
    scores = lax.psum(score, "y")

    partial = lax.all_to_all(
        partial.reshape(nj, local, cols), "z", 0, 0, tiled=True, axis_index_groups=stride2
    )
    hidden = jnp.sum(partial.astype(F32), axis=0)

    importance = (counts.astype(F32) * proj_grads.shape[1] / scores).astype(BF)

    target = dests[:, 0]
    dest_hot = (target[:, None] == jnp.arange(groups, dtype=jnp.int32)[None, :]).astype(jnp.int32)
    order = jnp.arange(local, dtype=jnp.int32)
    earlier = (order[:, None] > order[None, :]).astype(jnp.int32)
    rank = jnp.sum(jnp.dot(earlier, dest_hot) * dest_hot, axis=1)
    code = (2 * target + rank).astype(BF)

    lane = jnp.arange(128)[None, :]
    extra = jnp.where(lane == 0, importance[:, None], code[:, None])
    payload = jnp.concatenate([hidden.astype(BF), extra], 1)
    part = lax.all_gather(payload, "z", axis=0, tiled=True)

    codes = part[:, cols + 1].astype(jnp.int32)
    from_z = jnp.arange(nz * local, dtype=jnp.int32) // local
    place = (codes // 2) * (2 * groups) + (2 * from_z + c) * 2 + codes % 2

    slots = jnp.arange(4 * groups, dtype=jnp.int32) + 4 * z * groups
    pick = (slots[:, None] == place[None, :]).astype(BF)
    at_slots = jnp.dot(pick, part[:, :cols], preferred_element_type=F32)
    act = (at_slots * jax.nn.sigmoid(at_slots)).astype(BF).reshape(2, 2 * groups, cols)
    hf = part[:, :cols].astype(F32)
    imp = part[:, cols : cols + 1].astype(F32)
    slots = jnp.arange(2 * groups * groups, dtype=jnp.int32)
    hot = (slots[:, None] == place[None, :]).astype(BF)
    cot = lax.dot_general(hot, cot_slots, (((0,), (0,)), ((), ())), preferred_element_type=F32)
    squash = jax.nn.sigmoid(hf)
    grad = (imp * cot * squash * (1.0 + hf * (1.0 - squash))).astype(BF)
    grad = grad.reshape(nj, 2, local, cols)

    def product(core):
        out = 0.0
        for x_part, bb in ((x_same, b), (x_flip, 1 - b)):
            x_block = lax.dynamic_slice_in_dim(x_part, core * piece, piece, 1)
            grad_part = lax.dynamic_index_in_dim(grad, bb, 1, keepdims=False)
            out = out + lax.dot_general(
                x_block,
                grad_part.reshape(nj * local, cols),
                (((0,), (0,)), ((), ())),
                preferred_element_type=F32,
            )
        return out

    half = product(1 - c).astype(BF)
    half, act_sent = lax.optimization_barrier((half, at(act, 1 - c)))
    other = lax.ppermute(half, "c", SWAP)
    weight_grad = product(c) + other.astype(F32)
    activated = at(act, c) + lax.ppermute(act_sent, "c", SWAP)
    return activated, weight_grad


def solution(mesh, nx=4):
    dp, fsdp = mesh.devices.shape
    fine = Mesh(mesh.devices.reshape(nx, dp // nx, fsdp // 2, 2), ("x", "y", "z", "c"))
    dp, fsdp = ("x", "y"), ("z", "c")
    in_specs = (
        P(fsdp, None),
        P(dp, None),
        P(fsdp),
        P(fsdp, None),
        P(fsdp, None),
        P(fsdp, dp),
        P(fsdp, dp),
    )
    out_specs = (P(fsdp, dp), P(fsdp, dp))
    return jax.shard_map(shards, mesh=fine, in_specs=in_specs, out_specs=out_specs, check_vma=False)
```

```python
import jax
import jax.numpy as jnp
from jax import lax
from jax.sharding import Mesh, PartitionSpec as P

BF = jnp.bfloat16
F32 = jnp.float32
SWAP = [(0, 1), (1, 0)]


def both(flag, own, other, axis):
    return jnp.where(flag == 0, jnp.stack([own, other], axis), jnp.stack([other, own], axis))


def at(array, index, axis=0):
    return lax.dynamic_index_in_dim(array, index, axis, keepdims=False)


def shards(proj_grads, inv_factor, counts, dests, rows, weight, cotangent):
    nz = lax.axis_size("z")
    nj, groups = nz // 2, 2 * nz
    z, c = lax.axis_index("z"), lax.axis_index("c")
    b = z % 2
    local, width = rows.shape
    piece, cols = weight.shape
    quad = 4 * piece
    stride2 = [[2 * i + k for i in range(nj)] for k in range(2)]
    flip = [(i, i ^ 1) for i in range(nz)]

    def pair(x):
        return lax.ppermute(x, "z", flip)

    def core(x):
        return lax.ppermute(x, "c", SWAP)

    def exchange(x):
        return lax.all_to_all(x, "z", 0, 0, tiled=True, axis_index_groups=stride2)

    w_pair = both(b, weight, pair(weight), 0)
    w_quad = both(c, w_pair, core(w_pair), 1).reshape(quad, cols)

    came = exchange(rows.reshape(local, nj, quad).transpose(1, 0, 2))

    projected = lax.dot_general(
        proj_grads, inv_factor, (((1,), (1,)), ((), ())), preferred_element_type=F32
    )
    score = lax.psum(jnp.sum(projected * projected, axis=1), "x")
    came, score = lax.optimization_barrier((came, score))
    x_class = came.reshape(nj * local, quad)

    slots = cotangent.reshape(nj, 2, 2, 2, cols)
    slots = both(c, at(slots, c, 2), core(at(slots, 1 - c, 2)), 0)
    slots = both(b, at(slots, b, 2), pair(at(slots, 1 - b, 2)), 0)
    slots = slots.transpose(2, 0, 1, 3, 4).reshape(nj, 8, cols)

    target = dests[:, 0]
    dest_hot = (target[:, None] == jnp.arange(groups, dtype=jnp.int32)[None, :]).astype(jnp.int32)
    order = jnp.arange(local, dtype=jnp.int32)
    earlier = (order[:, None] > order[None, :]).astype(jnp.int32)
    rank = jnp.sum(jnp.dot(earlier, dest_hot) * dest_hot, axis=1)
    place = 2 * target + rank
    placer = (place[:, None] == jnp.arange(2 * groups, dtype=jnp.int32)[None, :]).astype(BF)

    partial = jnp.dot(x_class, w_quad, preferred_element_type=F32).astype(BF)
    sent = jnp.concatenate([partial.reshape(nj, local, cols), slots], 1)
    sent, score = lax.optimization_barrier((sent, score))
    came = exchange(sent)
    scores = lax.psum(score, "y")
    importance = (counts.astype(F32) * proj_grads.shape[1] / scores).astype(BF)
    x_blocks = x_class.reshape(nj * local, 2, 2 * piece)
    importance, x_sent = lax.optimization_barrier((importance, at(x_blocks, 1 - b, 1)))
    hidden = jnp.sum(came[:, :local].astype(F32), axis=0)
    cot = jnp.dot(placer, came[:, local:].reshape(2 * groups, cols), preferred_element_type=F32)
    squash = jax.nn.sigmoid(hidden)
    act = (hidden * squash).astype(BF)
    grad = importance[:, None].astype(F32) * cot * squash * (1.0 + hidden * (1.0 - squash))
    grad = jnp.broadcast_to(grad.astype(BF)[None], (nj, local, cols))
    act = lax.dot_general(placer, act, (((0,), (0,)), ((), ())), preferred_element_type=F32)
    act = act.astype(BF).reshape(nj, 8, cols)

    came = exchange(jnp.concatenate([grad, act], 1))
    grad = came[:, :local].reshape(nj * local, cols)
    grad_flip = pair(grad)
    x_same, x_flip = at(x_blocks, b, 1), pair(x_sent)

    def product(which):
        out = 0.0
        for x_part, g_part in ((x_same, grad), (x_flip, grad_flip)):
            out = out + lax.dot_general(
                lax.dynamic_slice_in_dim(x_part, which * piece, piece, 1),
                g_part,
                (((0,), (0,)), ((), ())),
                preferred_element_type=F32,
            )
        return out

    weight_grad = core(product(1 - c).astype(BF)).astype(F32) + product(c)

    act = came[:, local:].reshape(nj, 2, 2, 2, cols)
    act = both(b, at(act, b, 1), pair(at(act, 1 - b, 1)), 1)
    act = both(c, at(act, c, 2), core(at(act, 1 - c, 2)), 2)
    return act.reshape(2 * groups, cols), weight_grad


def solution(mesh, nx=4):
    dp, fsdp = mesh.devices.shape
    fine = Mesh(mesh.devices.reshape(nx, dp // nx, fsdp // 2, 2), ("x", "y", "z", "c"))
    dp, fsdp = ("x", "y"), ("z", "c")
    in_specs = (
        P(fsdp, None),
        P(dp, None),
        P(fsdp),
        P(fsdp, None),
        P(fsdp, None),
        P(fsdp, dp),
        P(fsdp, dp),
    )
    out_specs = (P(fsdp, dp), P(fsdp, dp))
    return jax.shard_map(shards, mesh=fine, in_specs=in_specs, out_specs=out_specs, check_vma=False)
```

```python
import jax
import jax.numpy as jnp
from jax import lax
from jax.sharding import Mesh, PartitionSpec as P

BF = jnp.bfloat16
F32 = jnp.float32
SWAP = [(0, 1), (1, 0)]


def both(flag, own, other, axis):
    return jnp.where(flag == 0, jnp.stack([own, other], axis), jnp.stack([other, own], axis))


def at(array, index, axis=0):
    return lax.dynamic_index_in_dim(array, index, axis, keepdims=False)


def shards(proj_grads, inv_factor, counts, dests, rows, weight, cotangent):
    nz = lax.axis_size("z")
    nj, groups = nz // 2, 2 * nz
    z, c = lax.axis_index("z"), lax.axis_index("c")
    b = z % 2
    local, width = rows.shape
    piece, cols = weight.shape
    quad = 4 * piece
    stride2 = [[2 * i + k for i in range(nj)] for k in range(2)]
    flip = [(i, i ^ 1) for i in range(nz)]

    def pair(x):
        return lax.ppermute(x, "z", flip)

    def core(x):
        return lax.ppermute(x, "c", SWAP)

    def exchange(x):
        return lax.all_to_all(x, "z", 0, 0, tiled=True, axis_index_groups=stride2)

    sent = rows.reshape(local, nj, quad).transpose(1, 0, 2)
    sent, w_flip = lax.optimization_barrier((sent, pair(weight)))
    w_pair = both(b, weight, w_flip, 0)
    w_quad = both(c, w_pair, core(w_pair), 1).reshape(quad, cols)

    came = exchange(sent)

    projected = lax.dot_general(
        proj_grads, inv_factor, (((1,), (1,)), ((), ())), preferred_element_type=F32
    )
    score = lax.psum(jnp.sum(projected * projected, axis=1), "x")
    came, score = lax.optimization_barrier((came, score))
    x_class = came.reshape(nj * local, quad)

    slots = cotangent.reshape(nj, 2, 2, 2, cols)
    slots = both(c, at(slots, c, 2), core(at(slots, 1 - c, 2)), 0)
    slots = both(b, at(slots, b, 2), pair(at(slots, 1 - b, 2)), 0)
    slots = slots.transpose(2, 0, 1, 3, 4).reshape(nj, 8, cols)

    target = dests[:, 0]
    dest_hot = (target[:, None] == jnp.arange(groups, dtype=jnp.int32)[None, :]).astype(jnp.int32)
    order = jnp.arange(local, dtype=jnp.int32)
    earlier = (order[:, None] > order[None, :]).astype(jnp.int32)
    rank = jnp.sum(jnp.dot(earlier, dest_hot) * dest_hot, axis=1)
    place = 2 * target + rank
    placer = (place[:, None] == jnp.arange(2 * groups, dtype=jnp.int32)[None, :]).astype(BF)

    partial = jnp.dot(x_class, w_quad, preferred_element_type=F32).astype(BF)
    sent = jnp.concatenate([partial.reshape(nj, local, cols), slots], 1)
    x_blocks = x_class.reshape(nj * local, 2, 2 * piece)
    sent, score, x_sent = lax.optimization_barrier((sent, score, at(x_blocks, 1 - b, 1)))
    x_same, x_flip = at(x_blocks, b, 1), pair(x_sent)
    came = exchange(sent)
    scores = lax.psum(score, "y")
    importance = (counts.astype(F32) * proj_grads.shape[1] / scores).astype(BF)
    hidden = jnp.sum(came[:, :local].astype(F32), axis=0)
    cot = jnp.dot(placer, came[:, local:].reshape(2 * groups, cols), preferred_element_type=F32)
    squash = jax.nn.sigmoid(hidden)
    act = (hidden * squash).astype(BF)
    grad = importance[:, None].astype(F32) * cot * squash * (1.0 + hidden * (1.0 - squash))
    grad = jnp.broadcast_to(grad.astype(BF)[None], (nj, local, cols))
    act = lax.dot_general(placer, act, (((0,), (0,)), ((), ())), preferred_element_type=F32)
    act = act.astype(BF).reshape(nj, 8, cols)

    sent, x_flip = lax.optimization_barrier((jnp.concatenate([grad, act], 1), x_flip))
    came = exchange(sent)
    grad = came[:, :local].reshape(nj * local, cols)
    grad_flip = pair(grad)

    def product(which, x_part, g_part):
        return lax.dot_general(
            lax.dynamic_slice_in_dim(x_part, which * piece, piece, 1),
            g_part,
            (((0,), (0,)), ((), ())),
            preferred_element_type=F32,
        )

    act = came[:, local:].reshape(nj, 2, 2, 2, cols)
    half, act_sent = lax.optimization_barrier((product(1 - c, x_same, grad), at(act, 1 - b, 1)))
    act = both(b, at(act, b, 1), pair(act_sent), 1)
    half = (half + product(1 - c, x_flip, grad_flip)).astype(BF)
    half, act_sent = lax.optimization_barrier((half, at(act, 1 - c, 2)))
    weight_grad = product(c, x_same, grad) + product(c, x_flip, grad_flip)
    weight_grad = core(half).astype(F32) + weight_grad
    act = both(c, at(act, c, 2), core(act_sent), 2)
    return act.reshape(2 * groups, cols), weight_grad


def solution(mesh, nx=4):
    dp, fsdp = mesh.devices.shape
    fine = Mesh(mesh.devices.reshape(nx, dp // nx, fsdp // 2, 2), ("x", "y", "z", "c"))
    dp, fsdp = ("x", "y"), ("z", "c")
    in_specs = (
        P(fsdp, None),
        P(dp, None),
        P(fsdp),
        P(fsdp, None),
        P(fsdp, None),
        P(fsdp, dp),
        P(fsdp, dp),
    )
    out_specs = (P(fsdp, dp), P(fsdp, dp))
    return jax.shard_map(shards, mesh=fine, in_specs=in_specs, out_specs=out_specs, check_vma=False)
```

```python
import jax
import jax.numpy as jnp
from jax import lax
from jax.sharding import Mesh, PartitionSpec as P

BF = jnp.bfloat16
F32 = jnp.float32
SWAP = [(0, 1), (1, 0)]


def both(flag, own, other, axis):
    return jnp.where(flag == 0, jnp.stack([own, other], axis), jnp.stack([other, own], axis))


def at(array, index, axis=0):
    return lax.dynamic_index_in_dim(array, index, axis, keepdims=False)


def shards(proj_grads, inv_factor, counts, dests, rows, weight, cotangent):
    nx, nz = lax.axis_size("x"), lax.axis_size("z")
    nj, groups = nz // 2, 2 * nz
    z, c = lax.axis_index("z"), lax.axis_index("c")
    b = z % 2
    local, width = rows.shape
    piece, cols = weight.shape
    quad = 4 * piece
    stride2 = [[2 * i + k for i in range(nj)] for k in range(2)]
    flip = [(i, i ^ 1) for i in range(nz)]

    def pair(x):
        return lax.ppermute(x, "z", flip)

    def core(x):
        return lax.ppermute(x, "c", SWAP)

    def exchange(x):
        return lax.all_to_all(x, "z", 0, 0, tiled=True, axis_index_groups=stride2)

    w_pair = both(b, weight, pair(weight), 0)
    w_quad = both(c, w_pair, core(w_pair), 1).reshape(quad, cols)

    share = local // nx
    sent = lax.dynamic_slice_in_dim(rows, lax.axis_index("x") * share, share, 0)
    came = exchange(sent.reshape(share, nj, quad).transpose(1, 0, 2))

    projected = lax.dot_general(
        proj_grads, inv_factor, (((1,), (1,)), ((), ())), preferred_element_type=F32
    )
    score = jnp.sum(projected * projected, axis=1)
    high = lax.reduce_precision(score, 8, 7)
    middle = lax.reduce_precision(score - high, 8, 7)
    low = score - high - middle
    thirds = jnp.concatenate([high, middle, low, jnp.zeros(quad - 3 * local, F32)]).astype(BF)
    thirds = jnp.broadcast_to(thirds[None, None, :], (1, share, quad))

    came = lax.all_gather(jnp.concatenate([came, thirds], 0), "x", axis=1, tiled=True)
    x_class = came[:nj].reshape(nj * local, quad)
    thirds = came[nj].reshape(nx, share, quad)[:, 0, : 3 * local].astype(F32)
    score = jnp.sum(thirds.reshape(nx * 3, local), axis=0)

    slots = cotangent.reshape(nj, 2, 2, 2, cols)
    slots = both(c, at(slots, c, 2), core(at(slots, 1 - c, 2)), 0)
    slots = both(b, at(slots, b, 2), pair(at(slots, 1 - b, 2)), 0)
    slots = slots.transpose(2, 0, 1, 3, 4).reshape(nj, 8, cols)

    target = dests[:, 0]
    dest_hot = (target[:, None] == jnp.arange(groups, dtype=jnp.int32)[None, :]).astype(jnp.int32)
    order = jnp.arange(local, dtype=jnp.int32)
    earlier = (order[:, None] > order[None, :]).astype(jnp.int32)
    rank = jnp.sum(jnp.dot(earlier, dest_hot) * dest_hot, axis=1)
    place = 2 * target + rank
    placer = (place[:, None] == jnp.arange(2 * groups, dtype=jnp.int32)[None, :]).astype(BF)

    partial = jnp.dot(x_class, w_quad, preferred_element_type=F32).astype(BF)
    sent = jnp.concatenate([partial.reshape(nj, local, cols), slots], 1)
    x_same, x_sent = (
        lax.dynamic_slice_in_dim(x_class, 2 * bb * piece, 2 * piece, 1) for bb in (b, 1 - b)
    )
    _, score, x_same, x_sent = lax.optimization_barrier(
        (partial[:8, :128], score, x_same, x_sent)
    )
    x_flip = pair(x_sent)
    came = exchange(sent)
    scores = lax.psum(score, "y")
    importance = (counts.astype(F32) * proj_grads.shape[1] / scores).astype(BF)
    hidden = jnp.sum(came[:, :local].astype(F32), axis=0)
    cot = jnp.dot(placer, came[:, local:].reshape(2 * groups, cols), preferred_element_type=F32)
    squash = jax.nn.sigmoid(hidden)
    act = (hidden * squash).astype(BF)
    grad = importance[:, None].astype(F32) * cot * squash * (1.0 + hidden * (1.0 - squash))
    grad = jnp.broadcast_to(grad.astype(BF)[None], (nj, local, cols))
    act = lax.dot_general(placer, act, (((0,), (0,)), ((), ())), preferred_element_type=F32)
    act = act.astype(BF).reshape(nj, 8, cols)

    sent, x_flip = lax.optimization_barrier((jnp.concatenate([grad, act], 1), x_flip))
    came = exchange(sent)
    grad = came[:, :local].reshape(nj * local, cols)
    grad_flip = pair(grad)

    def product(which, x_part, g_part):
        return lax.dot_general(
            lax.dynamic_slice_in_dim(x_part, which * piece, piece, 1),
            g_part,
            (((0,), (0,)), ((), ())),
            preferred_element_type=F32,
        )

    act = came[:, local:].reshape(nj, 2, 2, 2, cols)
    half, act_sent = lax.optimization_barrier((product(1 - c, x_same, grad), at(act, 1 - b, 1)))
    act = both(b, at(act, b, 1), pair(act_sent), 1)
    half = (half + product(1 - c, x_flip, grad_flip)).astype(BF)
    half, act_sent = lax.optimization_barrier((half, at(act, 1 - c, 2)))
    weight_grad = product(c, x_same, grad) + product(c, x_flip, grad_flip)
    weight_grad = core(half).astype(F32) + weight_grad
    act = both(c, at(act, c, 2), core(act_sent), 2)
    return act.reshape(2 * groups, cols), weight_grad


def solution(mesh, nx=4):
    dp, fsdp = mesh.devices.shape
    fine = Mesh(mesh.devices.reshape(nx, dp // nx, fsdp // 2, 2), ("x", "y", "z", "c"))
    dp, fsdp = ("x", "y"), ("z", "c")
    in_specs = (
        P(fsdp, None),
        P(dp, None),
        P(fsdp),
        P(fsdp, None),
        P(fsdp, None),
        P(fsdp, dp),
        P(fsdp, dp),
    )
    out_specs = (P(fsdp, dp), P(fsdp, dp))
    return jax.shard_map(shards, mesh=fine, in_specs=in_specs, out_specs=out_specs, check_vma=False)
```

```python
import jax
import jax.numpy as jnp
from jax import lax
from jax.sharding import Mesh, PartitionSpec as P

BF = jnp.bfloat16
F32 = jnp.float32
SWAP = [(0, 1), (1, 0)]


def both(flag, own, other, axis):
    return jnp.where(flag == 0, jnp.stack([own, other], axis), jnp.stack([other, own], axis))


def at(array, index, axis=0):
    return lax.dynamic_index_in_dim(array, index, axis, keepdims=False)


def shards(proj_grads, inv_factor, counts, dests, rows, weight, cotangent):
    nx, nz = lax.axis_size("x"), lax.axis_size("z")
    nj, groups = nz // 2, 2 * nz
    z, c = lax.axis_index("z"), lax.axis_index("c")
    b = z % 2
    local, width = rows.shape
    piece, cols = weight.shape
    quad = 4 * piece
    stride2 = [[2 * i + k for i in range(nj)] for k in range(2)]
    flip = [(i, i ^ 1) for i in range(nz)]

    def pair(x):
        return lax.ppermute(x, "z", flip)

    def core(x):
        return lax.ppermute(x, "c", SWAP)

    def exchange(x):
        return lax.all_to_all(x, "z", 0, 0, tiled=True, axis_index_groups=stride2)

    share = local // nx
    sent = lax.dynamic_slice_in_dim(rows, lax.axis_index("x") * share, share, 0)
    sent, weight = lax.optimization_barrier((sent, weight))
    came = exchange(sent.reshape(share, nj, quad).transpose(1, 0, 2))

    w_pair = both(b, weight, pair(weight), 0)
    w_quad = both(c, w_pair, core(w_pair), 1).reshape(quad, cols)

    projected = lax.dot_general(
        proj_grads, inv_factor, (((1,), (1,)), ((), ())), preferred_element_type=F32
    )
    score = jnp.sum(projected * projected, axis=1)
    high = lax.reduce_precision(score, 8, 7)
    middle = lax.reduce_precision(score - high, 8, 7)
    low = score - high - middle
    thirds = jnp.concatenate([high, middle, low, jnp.zeros(quad - 3 * local, F32)]).astype(BF)
    thirds = jnp.broadcast_to(thirds[None, None, :], (1, share, quad))

    came = lax.all_gather(jnp.concatenate([came, thirds], 0), "x", axis=1, tiled=True)
    x_class = came[:nj].reshape(nj * local, quad)
    thirds = came[nj].reshape(nx, share, quad)[:, 0, : 3 * local].astype(F32)
    score = jnp.sum(thirds.reshape(nx * 3, local), axis=0)

    slots = cotangent.reshape(nj, 2, 2, 2, cols)
    slots = both(c, at(slots, c, 2), core(at(slots, 1 - c, 2)), 0)
    slots = both(b, at(slots, b, 2), pair(at(slots, 1 - b, 2)), 0)
    slots = slots.transpose(2, 0, 1, 3, 4).reshape(nj, 8, cols)

    target = dests[:, 0]
    dest_hot = (target[:, None] == jnp.arange(groups, dtype=jnp.int32)[None, :]).astype(jnp.int32)
    order = jnp.arange(local, dtype=jnp.int32)
    earlier = (order[:, None] > order[None, :]).astype(jnp.int32)
    rank = jnp.sum(jnp.dot(earlier, dest_hot) * dest_hot, axis=1)
    place = 2 * target + rank
    placer = (place[:, None] == jnp.arange(2 * groups, dtype=jnp.int32)[None, :]).astype(BF)

    partial = jnp.dot(x_class, w_quad, preferred_element_type=F32).astype(BF)
    sent = jnp.concatenate([partial.reshape(nj, local, cols), slots], 1)
    x_same, x_sent = (
        lax.dynamic_slice_in_dim(x_class, 2 * bb * piece, 2 * piece, 1) for bb in (b, 1 - b)
    )
    _, score, x_same, x_sent = lax.optimization_barrier(
        (partial[:8, :128], score, x_same, x_sent)
    )
    came = exchange(sent)
    scores, x_sent = lax.optimization_barrier((lax.psum(score, "y"), x_sent))
    x_flip = pair(x_sent)
    importance = (counts.astype(F32) * proj_grads.shape[1] / scores).astype(BF)
    hidden = jnp.sum(came[:, :local].astype(F32), axis=0)
    cot = jnp.dot(placer, came[:, local:].reshape(2 * groups, cols), preferred_element_type=F32)
    squash = jax.nn.sigmoid(hidden)
    act = (hidden * squash).astype(BF)
    grad = importance[:, None].astype(F32) * cot * squash * (1.0 + hidden * (1.0 - squash))
    grad = jnp.broadcast_to(grad.astype(BF)[None], (nj, local, cols))
    act = lax.dot_general(placer, act, (((0,), (0,)), ((), ())), preferred_element_type=F32)
    act = act.astype(BF).reshape(nj, 8, cols)

    sent, x_flip = lax.optimization_barrier((jnp.concatenate([grad, act], 1), x_flip))
    came = exchange(sent)
    grad = came[:, :local].reshape(nj * local, cols)
    grad_flip = pair(grad)

    def product(which, x_part, g_part):
        return lax.dot_general(
            lax.dynamic_slice_in_dim(x_part, which * piece, piece, 1),
            g_part,
            (((0,), (0,)), ((), ())),
            preferred_element_type=F32,
        )

    act = came[:, local:].reshape(nj, 2, 2, 2, cols)
    half, act_sent = lax.optimization_barrier((product(1 - c, x_same, grad), at(act, 1 - b, 1)))
    act = both(b, at(act, b, 1), pair(act_sent), 1)
    half = (half + product(1 - c, x_flip, grad_flip)).astype(BF)
    half, act_sent = lax.optimization_barrier((half, at(act, 1 - c, 2)))
    weight_grad = product(c, x_same, grad) + product(c, x_flip, grad_flip)
    weight_grad = core(half).astype(F32) + weight_grad
    act = both(c, at(act, c, 2), core(act_sent), 2)
    return act.reshape(2 * groups, cols), weight_grad


def solution(mesh, nx=4):
    dp, fsdp = mesh.devices.shape
    fine = Mesh(mesh.devices.reshape(nx, dp // nx, fsdp // 2, 2), ("x", "y", "z", "c"))
    dp, fsdp = ("x", "y"), ("z", "c")
    in_specs = (
        P(fsdp, None),
        P(dp, None),
        P(fsdp),
        P(fsdp, None),
        P(fsdp, None),
        P(fsdp, dp),
        P(fsdp, dp),
    )
    out_specs = (P(fsdp, dp), P(fsdp, dp))
    return jax.shard_map(shards, mesh=fine, in_specs=in_specs, out_specs=out_specs, check_vma=False)
```

```python
import jax
import jax.numpy as jnp
from jax import lax
from jax.sharding import Mesh, PartitionSpec as P

BF = jnp.bfloat16
F32 = jnp.float32
SWAP = [(0, 1), (1, 0)]


def both(flag, own, other, axis):
    return jnp.where(flag == 0, jnp.stack([own, other], axis), jnp.stack([other, own], axis))


def at(array, index, axis=0):
    return lax.dynamic_index_in_dim(array, index, axis, keepdims=False)


def shards(proj_grads, inv_factor, counts, dests, rows, weight, cotangent):
    nx, nz = lax.axis_size("x"), lax.axis_size("z")
    nj, groups = nz // 2, 2 * nz
    z, c = lax.axis_index("z"), lax.axis_index("c")
    b = z % 2
    local, width = rows.shape
    piece, cols = weight.shape
    quad = 4 * piece
    stride2 = [[2 * i + k for i in range(nj)] for k in range(2)]
    flip = [(i, i ^ 1) for i in range(nz)]

    def pair(x):
        return lax.ppermute(x, "z", flip)

    def core(x):
        return lax.ppermute(x, "c", SWAP)

    def exchange(x):
        return lax.all_to_all(x, "z", 0, 0, tiled=True, axis_index_groups=stride2)

    w_pair = both(b, weight, pair(weight), 0)
    w_quad = both(c, w_pair, core(w_pair), 1).reshape(quad, cols)

    share = local // nx
    sent = lax.dynamic_slice_in_dim(rows, lax.axis_index("x") * share, share, 0)
    came = exchange(sent.reshape(share, nj, quad).transpose(1, 0, 2))

    projected = lax.dot_general(
        proj_grads, inv_factor, (((1,), (1,)), ((), ())), preferred_element_type=F32
    )
    score = jnp.sum(projected * projected, axis=1)
    high = lax.reduce_precision(score, 8, 7)
    middle = lax.reduce_precision(score - high, 8, 7)
    low = score - high - middle
    thirds = jnp.concatenate([high, middle, low, jnp.zeros(quad - 3 * local, F32)]).astype(BF)
    thirds = jnp.broadcast_to(thirds[None, None, :], (1, share, quad))

    sent = jnp.concatenate([came, thirds], 0)
    sent = jnp.broadcast_to(sent[None], (nx, nj + 1, share, quad))
    came = lax.all_to_all(sent, "x", 0, 0, tiled=True)
    came = came.transpose(1, 0, 2, 3).reshape(nj + 1, local, quad)
    x_class = came[:nj].reshape(nj * local, quad)
    thirds = came[nj].reshape(nx, share, quad)[:, 0, : 3 * local].astype(F32)
    score = jnp.sum(thirds.reshape(nx * 3, local), axis=0)

    slots = cotangent.reshape(nj, 2, 2, 2, cols)
    slots = both(c, at(slots, c, 2), core(at(slots, 1 - c, 2)), 0)
    slots = both(b, at(slots, b, 2), pair(at(slots, 1 - b, 2)), 0)
    slots = slots.transpose(2, 0, 1, 3, 4).reshape(nj, 8, cols)

    target = dests[:, 0]
    dest_hot = (target[:, None] == jnp.arange(groups, dtype=jnp.int32)[None, :]).astype(jnp.int32)
    order = jnp.arange(local, dtype=jnp.int32)
    earlier = (order[:, None] > order[None, :]).astype(jnp.int32)
    rank = jnp.sum(jnp.dot(earlier, dest_hot) * dest_hot, axis=1)
    place = 2 * target + rank
    placer = (place[:, None] == jnp.arange(2 * groups, dtype=jnp.int32)[None, :]).astype(BF)

    partial = jnp.dot(x_class, w_quad, preferred_element_type=F32).astype(BF)
    sent = jnp.concatenate([partial.reshape(nj, local, cols), slots], 1)
    x_same, x_sent = (
        lax.dynamic_slice_in_dim(x_class, 2 * bb * piece, 2 * piece, 1) for bb in (b, 1 - b)
    )
    _, score, x_same, x_sent = lax.optimization_barrier(
        (partial[:8, :128], score, x_same, x_sent)
    )
    x_flip = pair(x_sent)
    came = exchange(sent)
    scores = lax.psum(score, "y")
    importance = (counts.astype(F32) * proj_grads.shape[1] / scores).astype(BF)
    hidden = jnp.sum(came[:, :local].astype(F32), axis=0)
    cot = jnp.dot(placer, came[:, local:].reshape(2 * groups, cols), preferred_element_type=F32)
    squash = jax.nn.sigmoid(hidden)
    act = (hidden * squash).astype(BF)
    grad = importance[:, None].astype(F32) * cot * squash * (1.0 + hidden * (1.0 - squash))
    grad = jnp.broadcast_to(grad.astype(BF)[None], (nj, local, cols))
    act = lax.dot_general(placer, act, (((0,), (0,)), ((), ())), preferred_element_type=F32)
    act = act.astype(BF).reshape(nj, 8, cols)

    sent, x_flip = lax.optimization_barrier((jnp.concatenate([grad, act], 1), x_flip))
    came = exchange(sent)
    grad = came[:, :local].reshape(nj * local, cols)
    grad_flip = pair(grad)

    def product(which, x_part, g_part):
        return lax.dot_general(
            lax.dynamic_slice_in_dim(x_part, which * piece, piece, 1),
            g_part,
            (((0,), (0,)), ((), ())),
            preferred_element_type=F32,
        )

    act = came[:, local:].reshape(nj, 2, 2, 2, cols)
    half, act_sent = lax.optimization_barrier((product(1 - c, x_same, grad), at(act, 1 - b, 1)))
    act = both(b, at(act, b, 1), pair(act_sent), 1)
    half = (half + product(1 - c, x_flip, grad_flip)).astype(BF)
    half, act_sent = lax.optimization_barrier((half, at(act, 1 - c, 2)))
    weight_grad = product(c, x_same, grad) + product(c, x_flip, grad_flip)
    weight_grad = core(half).astype(F32) + weight_grad
    act = both(c, at(act, c, 2), core(act_sent), 2)
    return act.reshape(2 * groups, cols), weight_grad


def solution(mesh, nx=4):
    dp, fsdp = mesh.devices.shape
    fine = Mesh(mesh.devices.reshape(nx, dp // nx, fsdp // 2, 2), ("x", "y", "z", "c"))
    dp, fsdp = ("x", "y"), ("z", "c")
    in_specs = (
        P(fsdp, None),
        P(dp, None),
        P(fsdp),
        P(fsdp, None),
        P(fsdp, None),
        P(fsdp, dp),
        P(fsdp, dp),
    )
    out_specs = (P(fsdp, dp), P(fsdp, dp))
    return jax.shard_map(shards, mesh=fine, in_specs=in_specs, out_specs=out_specs, check_vma=False)
```
